32 devices in a mesh: layer: 2 (over core), feat: 16 (over z, y, x).
Axes of the slice: x: 2, y: 2, z: 4, core: 2. Of those that a mesh axis runs over, the one named last changes fastest.
Arguments:
- source: float32 [2, 64, 2048], P('layer', 'feat'), may hold values from -6 to 6
- w_enc: bfloat16 [2, 2048, 24576], P('layer', None, 'feat'), may hold values from -0.125 to 0.125
- b_enc: float32 [2, 24576], P('layer', 'feat'), may hold values from -3 to 3
- threshold: float32 [2, 24576], P('layer', 'feat'), may hold values from 0.2 to 2
- dec_self: bfloat16 [2, 24576, 2048], P('layer', 'feat'), may hold values from -0.0390625 to 0.0390625
- dec_next: bfloat16 [2, 24576, 2048], P('layer', 'feat'), may hold values from -0.0390625 to 0.0390625
- target: float32 [2, 64, 2048], P('layer', 'feat'), may hold values from -3 to 3
Outputs:
- residual: float32 [2, 64, 2048], P('layer', 'feat')
The draws below stay inside these ranges and needn't reach their ends.
All inputs are finite; a program needn't handle non-finite values.
Results may differ from the reference program's by a relative error of at most 0.0038.
Values may be sent and summed in bfloat16 or wider, within the bound.
No kernel may reach another device: no remote copies, remote signals or barrier semaphores. Data moves between devices by JAX's collectives and lax.ppermute only.
A program may use at most 64 MiB of HBM per device.

```python
import math
import jax
import jax.numpy as jnp
from jax import lax

D = 2048
F = 24576
ROWS = 64
LAYERS = 2


def block_scale(rng, dims, pieces, low, largest):
    loudness, own = 1.0, jax.random.fold_in(rng, 6)
    for axis_at, parts in pieces:
        steps = jnp.exp(jax.random.uniform(jax.random.fold_in(own, axis_at), (parts,), jnp.float32, low / len(pieces), largest / len(pieces)))
        loudness = loudness * jnp.repeat(steps, dims[axis_at] // parts).reshape([-1 if axis == axis_at else 1 for axis in range(len(dims))])
    return loudness


def scatter_about(key, extent, width, reach, cuts=(), dtype=jnp.bfloat16):
    drawn = width * jax.random.normal(key, extent, jnp.float32)
    if cuts:
        drawn = drawn * block_scale(key, extent, cuts, -0.22, 0.18)
    return jnp.clip(drawn, -reach, reach).astype(dtype)


def setup_inputs(seed: int = 0) -> dict:
    key_of = jax.random.split(jax.random.key(seed), 8)
    source = scatter_about(key_of[0], (LAYERS, ROWS, D), 1.0, 6.0, ((0, 2), (1, 16)), jnp.float32)
    w_enc = scatter_about(key_of[1], (LAYERS, D, F), D ** -0.5, 0.125, ((0, 2), (2, 16)))
    b_enc = scatter_about(key_of[2], (LAYERS, F), 0.5, 3.0, ((0, 2), (1, 16)), jnp.float32)
    threshold = jnp.clip(jnp.exp(math.log(2.0) - 2.3025851 * jax.random.uniform(key_of[3], (LAYERS, F), jnp.float32) ** block_scale(key_of[3], (LAYERS, F), ((0, 2), (1, 16)), -0.2, 0.2)), 0.2, 2.0)
    dec_self = scatter_about(key_of[4], (LAYERS, F, D), F ** -0.5, 0.0390625, ((0, 2), (1, 16)))
    dec_next = scatter_about(key_of[5], (LAYERS, F, D), F ** -0.5, 0.0390625, ((0, 2), (1, 16)))
    target = scatter_about(key_of[6], (LAYERS, ROWS, D), 0.5, 3.0, ((0, 2), (1, 16)), jnp.float32)
    return dict(source=source, w_enc=w_enc, b_enc=b_enc, threshold=threshold, dec_self=dec_self, dec_next=dec_next, target=target)


def section(inputs):
    rows, enc, bias, thr, dec_own, dec_after = inputs
    scale = lax.rsqrt(lax.optimization_barrier(jnp.mean(rows * rows, axis=1, keepdims=True)) + 1e-05)
    normed = (rows * scale).astype(jnp.bfloat16)
    pre = jnp.dot(normed, enc, preferred_element_type=jnp.float32) + bias
    codes = (pre * jax.nn.sigmoid((pre - thr) / 0.1)).astype(jnp.bfloat16)
    own = jnp.dot(codes, dec_own, preferred_element_type=jnp.float32)
    carried = jnp.dot(codes, dec_after, preferred_element_type=jnp.float32)
    return (own, carried)

def reference(source, w_enc, b_enc, threshold, dec_self, dec_next, target):
    own, carried = lax.map(section, (source, w_enc, b_enc, threshold, dec_self, dec_next))
    shifted = jnp.concatenate([jnp.zeros_like(carried[:1]), carried[:-1]], axis=0)
    return own + shifted - target
```

```python
import jax
import jax.numpy as jnp
from jax import lax
from jax.sharding import PartitionSpec as P


def body(source, w_enc, b_enc, threshold, dec_self, dec_next, target):
    feats = lax.axis_size("feat")
    layers = lax.axis_size("layer")
    rows = source[0]
    block, depth = rows.shape
    scale = lax.rsqrt(jnp.mean(rows * rows, axis=1, keepdims=True) + 1e-05)
    normed = (rows * scale).astype(jnp.bfloat16)
    spread = jnp.broadcast_to(normed[None], (feats, block, depth))
    gathered = lax.all_to_all(spread, "feat", 0, 0).reshape(feats * block, depth)
    pre = jnp.dot(gathered, w_enc[0], preferred_element_type=jnp.float32) + b_enc[0]
    codes = (pre * jax.nn.sigmoid((pre - threshold[0]) / 0.1)).astype(jnp.bfloat16)
    whole_next = jnp.dot(codes, dec_next[0], preferred_element_type=jnp.float32)
    ring = [(i, (i + 1) % layers) for i in range(layers)]
    arrived = lax.ppermute(whole_next.astype(jnp.bfloat16), "layer", ring)
    arrived = jnp.where(lax.axis_index("layer") > 0, arrived, jnp.zeros_like(arrived))
    own = jnp.dot(codes, dec_self[0], preferred_element_type=jnp.float32)
    part = (own + arrived.astype(jnp.float32)).astype(jnp.bfloat16)
    shares = lax.all_to_all(part.reshape(feats, block, depth), "feat", 0, 0)
    recon = jnp.sum(shares.astype(jnp.float32), axis=0)
    return (recon - target[0])[None]


def solution(mesh):
    return jax.shard_map(
        body,
        mesh=mesh,
        in_specs=(
            P("layer", "feat", None),
            P("layer", None, "feat"),
            P("layer", "feat"),
            P("layer", "feat"),
            P("layer", "feat", None),
            P("layer", "feat", None),
            P("layer", "feat", None),
        ),
        out_specs=P("layer", "feat", None),
        check_vma=False,
    )
```

```python
import jax
import jax.numpy as jnp
from jax import lax
from jax.experimental import pallas as pl
from jax.experimental.pallas import tpu as pltpu
from jax.sharding import PartitionSpec as P

VMEM = pl.BlockSpec(memory_space=pltpu.VMEM)
GRANT = 8 * 2**20


def call(kernel, out_shape, args, flops=0, moved=2**18):
    return pl.pallas_call(
        kernel,
        out_shape=out_shape,
        in_specs=[VMEM] * len(args),
        out_specs=jax.tree.map(lambda _: VMEM, out_shape),
        compiler_params=pltpu.CompilerParams(vmem_limit_bytes=GRANT),
        cost_estimate=pl.CostEstimate(flops=flops, bytes_accessed=moved, transcendentals=0),
    )(*args)


def spread_kernel(rows_ref, out_ref):
    rows = rows_ref[0]
    scale = lax.rsqrt(jnp.mean(rows * rows, axis=1, keepdims=True) + 1e-05)
    normed = (rows * scale).astype(jnp.bfloat16)
    out_ref[...] = jnp.broadcast_to(normed[None], out_ref.shape)


def encode_kernel(rows_ref, enc_ref, bias_ref, limit_ref, after_ref, codes_ref, carried_ref):
    rows = rows_ref[...].reshape(-1, rows_ref.shape[-1])
    pre = jnp.dot(rows, enc_ref[0], preferred_element_type=jnp.float32) + bias_ref[...]
    codes = (pre * jax.nn.sigmoid((pre - limit_ref[...]) / 0.1)).astype(jnp.bfloat16)
    codes_ref[...] = codes
    last = lax.axis_index("layer") == lax.axis_size("layer") - 1

    @pl.when(last)
    def _():
        carried_ref[...] = jnp.zeros_like(carried_ref)

    @pl.when(jnp.logical_not(last))
    def _():
        carried = jnp.dot(codes, after_ref[0], preferred_element_type=jnp.float32)
        carried_ref[...] = carried.astype(jnp.bfloat16)


def decode_kernel(codes_ref, dec_ref, own_ref):
    own_ref[...] = jnp.dot(codes_ref[...], dec_ref[0], preferred_element_type=jnp.float32)


def join_kernel(own_ref, arrived_ref, part_ref):
    part = own_ref[...] + arrived_ref[...].astype(jnp.float32)
    part_ref[...] = part.astype(jnp.bfloat16).reshape(part_ref.shape)


def finish_kernel(shares_ref, target_ref, out_ref):
    out_ref[0] = jnp.sum(shares_ref[...].astype(jnp.float32), axis=0) - target_ref[0]


def body(source, w_enc, b_enc, threshold, dec_self, dec_next, target):
    feats = lax.axis_size("feat")
    layers = lax.axis_size("layer")
    _, block, depth = source.shape
    width = w_enc.shape[2]
    rows = feats * block
    work = 2 * rows * depth * width
    half, full = jnp.bfloat16, jnp.float32
    shape = jax.ShapeDtypeStruct
    spread = call(spread_kernel, shape((feats, block, depth), half), (source,), 2**36, 2**27)
    gathered = lax.all_to_all(spread, "feat", 0, 0)
    codes, carried = call(
        encode_kernel,
        (shape((rows, width), half), shape((rows, depth), half)),
        (gathered, w_enc, b_enc, threshold, dec_next),
        2 * work,
    )
    arrived = lax.ppermute(carried, "layer", [(i, (i + 1) % layers) for i in range(layers)])
    own = call(decode_kernel, shape((rows, depth), full), (codes, dec_self), work)
    part = call(join_kernel, shape((feats, block, depth), half), (own, arrived))
    shares = lax.all_to_all(part, "feat", 0, 0)
    return call(finish_kernel, shape(target.shape, full), (shares, target))


def solution(mesh):
    return jax.shard_map(
        body,
        mesh=mesh,
        in_specs=(
            P("layer", "feat", None),
            P("layer", None, "feat"),
            P("layer", "feat"),
            P("layer", "feat"),
            P("layer", "feat", None),
            P("layer", "feat", None),
            P("layer", "feat", None),
        ),
        out_specs=P("layer", "feat", None),
        check_vma=False,
    )
```

```python
import jax
import jax.numpy as jnp
from jax import lax
from jax.experimental import pallas as pl
from jax.experimental.pallas import tpu as pltpu
from jax.sharding import PartitionSpec as P

VMEM = pl.BlockSpec(memory_space=pltpu.VMEM)
GRANT = 8 * 2**20
RADIX = 4


def call(kernel, out_shape, args, flops=0, moved=2**18):
    return pl.pallas_call(
        kernel,
        out_shape=out_shape,
        in_specs=[VMEM] * len(args),
        out_specs=jax.tree.map(lambda _: VMEM, out_shape),
        compiler_params=pltpu.CompilerParams(vmem_limit_bytes=GRANT),
        cost_estimate=pl.CostEstimate(flops=flops, bytes_accessed=moved, transcendentals=0),
    )(*args)


def normalise_kernel(rows_ref, out_ref):
    rows = rows_ref[0]
    scale = lax.rsqrt(jnp.mean(rows * rows, axis=1, keepdims=True) + 1e-05)
    out_ref[...] = (rows * scale).astype(jnp.bfloat16)


def stack_kernel(*refs):
    *block_refs, out_ref = refs
    whole = jnp.concatenate([ref[...].astype(jnp.float32) for ref in block_refs], axis=0)
    out_ref[...] = whole.astype(jnp.bfloat16)


def encode_kernel(*refs):
    *block_refs, enc_ref, bias_ref, limit_ref, codes_ref = refs
    rows = jnp.concatenate([ref[...] for ref in block_refs], axis=0)
    pre = jnp.dot(rows, enc_ref[0], preferred_element_type=jnp.float32) + bias_ref[...]
    codes_ref[...] = (pre * jax.nn.sigmoid((pre - limit_ref[...]) / 0.1)).astype(jnp.bfloat16)


def decode_kernel(codes_ref, dec_ref, own_ref):
    own_ref[...] = jnp.dot(codes_ref[...], dec_ref[0], preferred_element_type=jnp.float32)


def cut(total, part_refs):
    size = part_refs[0].shape[0]
    for i, part_ref in enumerate(part_refs):
        part_ref[...] = total[i * size : (i + 1) * size].astype(jnp.bfloat16)


def join_kernel(own_ref, before_ref, dec_ref, *part_refs):
    first = lax.axis_index("layer") == 0

    @pl.when(first)
    def _():
        cut(own_ref[...], part_refs)

    @pl.when(jnp.logical_not(first))
    def _():
        carried = jnp.dot(before_ref[...], dec_ref[0], preferred_element_type=jnp.float32)
        cut(own_ref[...] + carried, part_refs)


def added(block_refs):
    return sum(ref[...].astype(jnp.float32) for ref in block_refs)


def split_kernel(count, *refs):
    cut(added(refs[:count]), refs[count:])


def finish_kernel(*refs):
    *block_refs, target_ref, out_ref = refs
    out_ref[0] = added(block_refs) - target_ref[0]


def digits(count):
    assert count & (count - 1) == 0
    found, stride = [], 1
    while stride < count:
        radix = min(RADIX, count // stride)
        found.append((stride, radix))
        stride *= radix
    return found or [(1, 1)]


def body(source, w_enc, b_enc, threshold, dec_self, dec_next, target):
    feats = lax.axis_size("feat")
    layers = lax.axis_size("layer")
    _, block, depth = source.shape
    width = w_enc.shape[2]
    rows = feats * block
    work = 2 * rows * depth * width
    half, full = jnp.bfloat16, jnp.float32
    shape = jax.ShapeDtypeStruct
    steps = digits(feats)

    def swap(value, flip):
        return lax.ppermute(value, "feat", [(i, i ^ flip) for i in range(feats)])

    def onward(value):
        return lax.ppermute(value, "layer", [(i, (i + 1) % layers) for i in range(layers)])

    arrived_dec = onward(dec_next)

    line = call(normalise_kernel, shape((block, depth), half), (source,), 2**36, 2**27)
    for at, (stride, radix) in enumerate(reversed(steps)):
        blocks = [line] + [swap(line, stride * j) for j in range(1, radix)]
        if at < len(steps) - 1:
            line = call(stack_kernel, shape((radix * line.shape[0], depth), half), blocks, 2**34)

    codes = call(encode_kernel, shape((rows, width), half), (*blocks, w_enc, b_enc, threshold), work)
    before = onward(codes)
    own = call(decode_kernel, shape((rows, depth), full), (codes, dec_self), work)

    size = rows // steps[0][1]
    parts = call(join_kernel, (shape((size, depth), half),) * steps[0][1], (own, before, arrived_dec), work)
    for at, (stride, radix) in enumerate(steps):
        blocks = [parts[0]] + [swap(parts[j], stride * j) for j in reversed(range(1, radix))]
        if at < len(steps) - 1:
            following = steps[at + 1][1]
            size //= following
            kernel = lambda *refs, count=radix: split_kernel(count, *refs)
            parts = call(kernel, (shape((size, depth), half),) * following, blocks)
    return call(finish_kernel, shape(target.shape, full), (*blocks, target))


def solution(mesh):
    return jax.shard_map(
        body,
        mesh=mesh,
        in_specs=(
            P("layer", "feat", None),
            P("layer", None, "feat"),
            P("layer", "feat"),
            P("layer", "feat"),
            P("layer", "feat", None),
            P("layer", "feat", None),
            P("layer", "feat", None),
        ),
        out_specs=P("layer", "feat", None),
        check_vma=False,
    )
```

```python
import functools

import jax
import jax.numpy as jnp
from jax import lax
from jax.experimental import pallas as pl
from jax.experimental.pallas import tpu as pltpu
from jax.sharding import PartitionSpec as P

VMEM = pl.BlockSpec(memory_space=pltpu.VMEM)
GRANT = 8 * 2**20
RADIX = 4
TALL = 128


def call(kernel, out_shape, args, flops=0, moved=2**18):
    return pl.pallas_call(
        kernel,
        out_shape=out_shape,
        in_specs=[VMEM] * len(args),
        out_specs=jax.tree.map(lambda _: VMEM, out_shape),
        compiler_params=pltpu.CompilerParams(vmem_limit_bytes=GRANT),
        cost_estimate=pl.CostEstimate(flops=flops, bytes_accessed=moved, transcendentals=0),
    )(*args)


def dot(rows, weights):
    count = rows.shape[0]
    short = -count % TALL
    if short:
        rows = jnp.concatenate([rows, jnp.zeros((short, rows.shape[1]), rows.dtype)], axis=0)
    return jnp.dot(rows, weights, preferred_element_type=jnp.float32)[:count]


def scaled(rows):
    return rows * lax.rsqrt(jnp.mean(rows * rows, axis=1, keepdims=True) + 1e-05)


def own_kernel(rows_ref, out_ref):
    out_ref[...] = scaled(rows_ref[0])


def normalise_kernel(order, own_ref, *refs):
    *block_refs, out_ref = refs
    rows = [own_ref[...]] + [scaled(block_refs[order.index(j)][0]) for j in sorted(order)]
    out_ref[...] = jnp.concatenate(rows, axis=0).astype(jnp.bfloat16)


def stack_kernel(*refs):
    *block_refs, out_ref = refs
    whole = jnp.concatenate([ref[...].astype(jnp.float32) for ref in block_refs], axis=0)
    out_ref[...] = whole.astype(jnp.bfloat16)


def encode_kernel(*refs):
    *block_refs, enc_ref, bias_ref, limit_ref, codes_ref = refs
    rows = jnp.concatenate([ref[...] for ref in block_refs], axis=0)
    pre = dot(rows, enc_ref[0]) + bias_ref[...]
    codes_ref[...] = (pre * jax.nn.sigmoid((pre - limit_ref[...]) / 0.1)).astype(jnp.bfloat16)


def decode_kernel(codes_ref, dec_ref, own_ref):
    own_ref[...] = dot(codes_ref[...], dec_ref[0])


def cut(total, part_refs):
    size = part_refs[0].shape[0]
    for i, part_ref in enumerate(part_refs):
        part_ref[...] = total[i * size : (i + 1) * size].astype(jnp.bfloat16)


def join_kernel(own_ref, before_ref, dec_ref, *part_refs):
    first = lax.axis_index("layer") == 0

    @pl.when(first)
    def _():
        cut(own_ref[...], part_refs)

    @pl.when(jnp.logical_not(first))
    def _():
        carried = dot(before_ref[...], dec_ref[0])
        cut(own_ref[...] + carried, part_refs)


def added(block_refs):
    return sum(ref[...].astype(jnp.float32) for ref in block_refs)


def split_kernel(count, *refs):
    cut(added(refs[:count]), refs[count:])


def finish_kernel(*refs):
    *block_refs, target_ref, out_ref = refs
    out_ref[0] = added(block_refs) - target_ref[0]


def digits(count):
    assert count & (count - 1) == 0
    found, stride = [], 1
    while stride < count:
        radix = min(RADIX, count // stride)
        found.append((stride, radix))
        stride *= radix
    return found or [(1, 1)]


def body(source, w_enc, b_enc, threshold, dec_self, dec_next, target):
    feats = lax.axis_size("feat")
    layers = lax.axis_size("layer")
    _, block, depth = source.shape
    width = w_enc.shape[2]
    rows = feats * block
    work = 2 * rows * depth * width
    half, full = jnp.bfloat16, jnp.float32
    shape = jax.ShapeDtypeStruct
    steps = digits(feats)

    def swap(value, flip):
        return lax.ppermute(value, "feat", [(i, i ^ flip) for i in range(feats)])

    def onward(value):
        return lax.ppermute(value, "layer", [(i, (i + 1) % layers) for i in range(layers)])

    arrived_dec = onward(dec_next)

    *others, (stride, radix) = steps
    order = [radix - 1, *range(1, radix - 1)] if radix > 1 else []
    blocks = [swap(source, stride * j) for j in order]
    own = call(own_kernel, shape((block, depth), full), (source,), 2**36, 2**27)
    size = radix * block
    kernel = functools.partial(normalise_kernel, order)
    blocks = [call(kernel, shape((size, depth), half), [own] + blocks, 2**34)]
    for stride, radix in reversed(others):
        if len(blocks) > 1:
            blocks = [call(stack_kernel, shape((size, depth), half), blocks, 2**34)]
        blocks += [swap(blocks[0], stride * j) for j in range(1, radix)]
        size *= radix

    codes = call(encode_kernel, shape((rows, width), half), (*blocks, w_enc, b_enc, threshold), work)
    before = onward(codes)
    own = call(decode_kernel, shape((rows, depth), full), (codes, dec_self), work)

    size = rows // steps[0][1]
    parts = call(join_kernel, (shape((size, depth), half),) * steps[0][1], (own, before, arrived_dec), work)
    for at, (stride, radix) in enumerate(steps):
        blocks = [parts[0]] + [swap(parts[j], stride * j) for j in reversed(range(1, radix))]
        if at < len(steps) - 1:
            following = steps[at + 1][1]
            size //= following
            kernel = functools.partial(split_kernel, radix)
            parts = call(kernel, (shape((size, depth), half),) * following, blocks)
    return call(finish_kernel, shape(target.shape, full), (*blocks, target))


def solution(mesh):
    return jax.shard_map(
        body,
        mesh=mesh,
        in_specs=(
            P("layer", "feat", None),
            P("layer", None, "feat"),
            P("layer", "feat"),
            P("layer", "feat"),
            P("layer", "feat", None),
            P("layer", "feat", None),
            P("layer", "feat", None),
        ),
        out_specs=P("layer", "feat", None),
        check_vma=False,
    )
```

```python
import functools

import jax
import jax.numpy as jnp
import numpy as np
from jax import lax
from jax.experimental import pallas as pl
from jax.experimental.pallas import tpu as pltpu
from jax.sharding import PartitionSpec as P

VMEM = pl.BlockSpec(memory_space=pltpu.VMEM)
GRANT = 8 * 2**20
RADIX = 4
TALL = 128


def call(kernel, out_shape, args, flops=0, moved=2**18):
    return pl.pallas_call(
        kernel,
        out_shape=out_shape,
        in_specs=[VMEM] * len(args),
        out_specs=jax.tree.map(lambda _: VMEM, out_shape),
        compiler_params=pltpu.CompilerParams(vmem_limit_bytes=GRANT),
        cost_estimate=pl.CostEstimate(flops=flops, bytes_accessed=moved, transcendentals=0),
    )(*args)


def dot(rows, weights):
    count = rows.shape[0]
    short = -count % TALL
    if short:
        rows = jnp.concatenate([rows, jnp.zeros((short, rows.shape[1]), rows.dtype)], axis=0)
    return jnp.dot(rows, weights, preferred_element_type=jnp.float32)[:count]


def scaled(rows):
    return rows * lax.rsqrt(jnp.mean(rows * rows, axis=1, keepdims=True) + 1e-05)


def own_kernel(rows_ref, out_ref):
    out_ref[...] = scaled(rows_ref[0])


def normalise_kernel(order, own_ref, *refs):
    *block_refs, out_ref = refs
    rows = [own_ref[...]] + [scaled(block_refs[order.index(j)][0]) for j in sorted(order)]
    out_ref[...] = jnp.concatenate(rows, axis=0).astype(jnp.bfloat16)


def stack_kernel(*refs):
    *block_refs, out_ref = refs
    whole = jnp.concatenate([ref[...].astype(jnp.float32) for ref in block_refs], axis=0)
    out_ref[...] = whole.astype(jnp.bfloat16)


def encode_kernel(*refs):
    *block_refs, enc_ref, bias_ref, limit_ref, codes_ref = refs
    rows = jnp.concatenate([ref[...] for ref in block_refs], axis=0)
    pre = dot(rows, enc_ref[0]) + bias_ref[...]
    codes_ref[...] = (pre * jax.nn.sigmoid((pre - limit_ref[...]) / 0.1)).astype(jnp.bfloat16)


def decode_kernel(codes_ref, dec_ref, own_ref):
    own_ref[...] = dot(codes_ref[...], dec_ref[0])


def cut(total, part_refs):
    size = part_refs[0].shape[0]
    for i, part_ref in enumerate(part_refs):
        part_ref[...] = total[i * size : (i + 1) * size].astype(jnp.bfloat16)


def join_kernel(places, own_ref, before_ref, dec_ref, *part_refs):
    first = lax.axis_index("layer") == 0

    @pl.when(first)
    def _():
        cut(own_ref[...], part_refs)

    @pl.when(jnp.logical_not(first))
    def _():
        carried = dot(before_ref[...], dec_ref[0])
        block = carried.shape[0] // len(places)
        carried = jnp.concatenate([carried[i * block : (i + 1) * block] for i in places], axis=0)
        cut(own_ref[...] + carried, part_refs)


def added(block_refs):
    return sum(ref[...].astype(jnp.float32) for ref in block_refs)


def split_kernel(count, *refs):
    cut(added(refs[:count]), refs[count:])


def finish_kernel(*refs):
    *block_refs, target_ref, out_ref = refs
    out_ref[0] = added(block_refs) - target_ref[0]


def digits(count):
    assert count & (count - 1) == 0
    found, stride = [], 1
    while stride < count:
        radix = min(RADIX, count // stride)
        found.append((stride, radix))
        stride *= radix
    return found or [(1, 1)]


def body(source, w_enc, b_enc, threshold, dec_self, dec_next, target):
    feats = lax.axis_size("feat")
    layers = lax.axis_size("layer")
    _, block, depth = source.shape
    width = w_enc.shape[2]
    rows = feats * block
    work = 2 * rows * depth * width
    half, full = jnp.bfloat16, jnp.float32
    shape = jax.ShapeDtypeStruct
    steps = digits(feats)

    radices = [radix for _, radix in steps]
    turned = radices == radices[::-1]
    strides = [[stride for stride, _ in steps]] * 2
    if turned:
        strides = [strides[0], strides[0][::-1]]
    places = np.arange(feats).reshape(radices)
    places = [int(i) for i in (places.T if turned else places).ravel()]

    def swap(value, stage, j):
        flips = [strides[k % 2][stage] * j for k in range(layers)]
        pairs = [(k * feats + i, k * feats + (i ^ flips[k])) for k in range(layers) for i in range(feats)]
        return lax.ppermute(value, ("layer", "feat"), pairs)

    def onward(value):
        return lax.ppermute(value, "layer", [(i, (i + 1) % layers) for i in range(layers)])

    arrived_dec = onward(dec_next)

    last, radix = len(steps) - 1, radices[-1]
    order = [radix - 1, *range(1, radix - 1)] if radix > 1 else []
    blocks = [swap(source, last, j) for j in order]
    own = call(own_kernel, shape((block, depth), full), (source,), 2**36, 2**27)
    size = radix * block
    kernel = functools.partial(normalise_kernel, order)
    blocks = [call(kernel, shape((size, depth), half), [own] + blocks, 2**34)]
    for stage in reversed(range(last)):
        if len(blocks) > 1:
            blocks = [call(stack_kernel, shape((size, depth), half), blocks, 2**34)]
        blocks += [swap(blocks[0], stage, j) for j in range(1, radices[stage])]
        size *= radices[stage]

    codes = call(encode_kernel, shape((rows, width), half), (*blocks, w_enc, b_enc, threshold), work)
    before = onward(codes)
    own = call(decode_kernel, shape((rows, depth), full), (codes, dec_self), work)

    size = rows // radices[0]
    kernel = functools.partial(join_kernel, places)
    parts = call(kernel, (shape((size, depth), half),) * radices[0], (own, before, arrived_dec), work)
    for stage, radix in enumerate(radices):
        blocks = [parts[0]] + [swap(parts[j], stage, j) for j in reversed(range(1, radix))]
        if stage < last:
            size //= radices[stage + 1]
            kernel = functools.partial(split_kernel, radix)
            parts = call(kernel, (shape((size, depth), half),) * radices[stage + 1], blocks)
    return call(finish_kernel, shape(target.shape, full), (*blocks, target))


def solution(mesh):
    return jax.shard_map(
        body,
        mesh=mesh,
        in_specs=(
            P("layer", "feat", None),
            P("layer", None, "feat"),
            P("layer", "feat"),
            P("layer", "feat"),
            P("layer", "feat", None),
            P("layer", "feat", None),
            P("layer", "feat", None),
        ),
        out_specs=P("layer", "feat", None),
        check_vma=False,
    )
```

```python
import functools

import jax
import jax.numpy as jnp
import numpy as np
from jax import lax
from jax.experimental import pallas as pl
from jax.experimental.pallas import tpu as pltpu
from jax.sharding import PartitionSpec as P

VMEM = pl.BlockSpec(memory_space=pltpu.VMEM)
GRANT = 8 * 2**20
RADIX = 4
TALL = 128


def call(kernel, out_shape, args, flops=0, moved=2**18, aliases=()):
    return pl.pallas_call(
        kernel,
        out_shape=out_shape,
        input_output_aliases=dict(aliases),
        in_specs=[VMEM] * len(args),
        out_specs=jax.tree.map(lambda _: VMEM, out_shape),
        compiler_params=pltpu.CompilerParams(vmem_limit_bytes=GRANT),
        cost_estimate=pl.CostEstimate(flops=flops, bytes_accessed=moved, transcendentals=0),
    )(*args)


def dot(rows, weights):
    count = rows.shape[0]
    short = -count % TALL
    if short:
        rows = jnp.concatenate([rows, jnp.zeros((short, rows.shape[1]), rows.dtype)], axis=0)
    return jnp.dot(rows, weights, preferred_element_type=jnp.float32)[:count]


def scaled(rows):
    return rows * lax.rsqrt(jnp.mean(rows * rows, axis=1, keepdims=True) + 1e-05)


def own_kernel(rows_ref, out_ref):
    out_ref[...] = scaled(rows_ref[0])


def normalise_kernel(order, own_ref, *refs):
    *block_refs, out_ref = refs
    rows = [own_ref[...]] + [scaled(block_refs[order.index(j)][0]) for j in sorted(order)]
    out_ref[...] = jnp.concatenate(rows, axis=0).astype(jnp.bfloat16)


def stack_kernel(*refs):
    *block_refs, out_ref = refs
    whole = jnp.concatenate([ref[...].astype(jnp.float32) for ref in block_refs], axis=0)
    out_ref[...] = whole.astype(jnp.bfloat16)


def encode_kernel(*refs):
    *block_refs, enc_ref, bias_ref, limit_ref, codes_ref = refs
    rows = jnp.concatenate([ref[...] for ref in block_refs], axis=0)
    pre = dot(rows, enc_ref[0]) + bias_ref[...]
    codes_ref[...] = (pre * jax.nn.sigmoid((pre - limit_ref[...]) / 0.1)).astype(jnp.bfloat16)


def decode_kernel(codes_ref, dec_ref, own_ref, *part_refs):
    own = dot(codes_ref[...], dec_ref[0])
    own_ref[...] = own
    cut(own, part_refs)


def cut(total, part_refs):
    size = part_refs[0].shape[0]
    for i, part_ref in enumerate(part_refs):
        part_ref[...] = total[i * size : (i + 1) * size].astype(jnp.bfloat16)


def join_kernel(places, own_ref, before_ref, dec_ref, *refs):
    part_refs = refs[len(refs) // 2 :]

    @pl.when(lax.axis_index("layer") > 0)
    def _():
        carried = dot(before_ref[...], dec_ref[0])
        block = carried.shape[0] // len(places)
        carried = jnp.concatenate([carried[i * block : (i + 1) * block] for i in places], axis=0)
        cut(own_ref[...] + carried, part_refs)


def added(block_refs):
    return sum(ref[...].astype(jnp.float32) for ref in block_refs)


def gather_up_kernel(*refs):
    *block_refs, out_ref = refs
    out_ref[...] = added(block_refs)


def add_kernel(*refs):
    *block_refs, out_ref = refs
    out_ref[...] = added(block_refs)


def split_kernel(count, *refs):
    cut(added(refs[:count]), refs[count:])


def finish_kernel(*refs):
    *block_refs, target_ref, out_ref = refs
    out_ref[0] = added(block_refs) - target_ref[0]


def digits(count):
    assert count & (count - 1) == 0
    found, stride = [], 1
    while stride < count:
        radix = min(RADIX, count // stride)
        found.append((stride, radix))
        stride *= radix
    return found or [(1, 1)]


def body(source, w_enc, b_enc, threshold, dec_self, dec_next, target):
    feats = lax.axis_size("feat")
    layers = lax.axis_size("layer")
    _, block, depth = source.shape
    width = w_enc.shape[2]
    rows = feats * block
    work = 2 * rows * depth * width
    half, full = jnp.bfloat16, jnp.float32
    shape = jax.ShapeDtypeStruct
    steps = digits(feats)

    radices = [radix for _, radix in steps]
    turned = radices == radices[::-1]
    strides = [[stride for stride, _ in steps]] * 2
    if turned:
        strides = [strides[0], strides[0][::-1]]
    places = np.arange(feats).reshape(radices)
    places = [int(i) for i in (places.T if turned else places).ravel()]

    def swap(value, stage, j):
        flips = [strides[k % 2][stage] * j for k in range(layers)]
        pairs = [(k * feats + i, k * feats + (i ^ flips[k])) for k in range(layers) for i in range(feats)]
        return lax.ppermute(value, ("layer", "feat"), pairs)

    def onward(value):
        return lax.ppermute(value, "layer", [(i, (i + 1) % layers) for i in range(layers)])

    arrived_dec = onward(dec_next)

    last, radix = len(steps) - 1, radices[-1]
    order = [radix - 1, *range(1, radix - 1)] if radix > 1 else []
    blocks = [swap(source, last, j) for j in order]
    own = call(own_kernel, shape((block, depth), full), (source,), 2**36, 2**27)
    size = radix * block
    kernel = functools.partial(normalise_kernel, order)
    blocks = [call(kernel, shape((size, depth), half), [own] + blocks, 2**34)]
    for stage in reversed(range(last)):
        if len(blocks) > 1:
            blocks = [call(stack_kernel, shape((size, depth), half), blocks, 2**34)]
        blocks += [swap(blocks[0], stage, j) for j in range(1, radices[stage])]
        size *= radices[stage]

    codes = call(encode_kernel, shape((rows, width), half), (*blocks, w_enc, b_enc, threshold), work)
    before = onward(codes)
    size = rows // radices[0]
    pieces = (shape((size, depth), half),) * radices[0]
    own, *parts = call(decode_kernel, (shape((rows, depth), full), *pieces), (codes, dec_self), work)
    kernel = functools.partial(join_kernel, places)
    operands = (own, before, arrived_dec, *parts)
    parts = call(kernel, pieces, operands, work, aliases=[(3 + i, i) for i in range(radices[0])])
    for stage, radix in enumerate(radices):
        blocks = [parts[0]] + [swap(parts[j], stage, j) for j in reversed(range(1, radix))]
        if len(blocks) > 2:
            sofar = call(add_kernel, shape(parts[0].shape, full), blocks[:2])
            blocks = [sofar] + blocks[2:]
        if stage < last:
            size //= radices[stage + 1]
            kernel = functools.partial(split_kernel, len(blocks))
            parts = call(kernel, (shape((size, depth), half),) * radices[stage + 1], blocks)
    return call(finish_kernel, shape(target.shape, full), (*blocks, target))


def solution(mesh):
    return jax.shard_map(
        body,
        mesh=mesh,
        in_specs=(
            P("layer", "feat", None),
            P("layer", None, "feat"),
            P("layer", "feat"),
            P("layer", "feat"),
            P("layer", "feat", None),
            P("layer", "feat", None),
            P("layer", "feat", None),
        ),
        out_specs=P("layer", "feat", None),
        check_vma=False,
    )
```

```python
import functools

import jax
import jax.numpy as jnp
import numpy as np
from jax import lax
from jax.experimental import pallas as pl
from jax.experimental.pallas import tpu as pltpu
from jax.sharding import PartitionSpec as P

VMEM = pl.BlockSpec(memory_space=pltpu.VMEM)
GRANT = 8 * 2**20
RADIX = 4
TALL = 128


def call(kernel, out_shape, args, flops=0, moved=2**18, aliases=()):
    return pl.pallas_call(
        kernel,
        out_shape=out_shape,
        input_output_aliases=dict(aliases),
        in_specs=[VMEM] * len(args),
        out_specs=jax.tree.map(lambda _: VMEM, out_shape),
        compiler_params=pltpu.CompilerParams(vmem_limit_bytes=GRANT),
        cost_estimate=pl.CostEstimate(flops=flops, bytes_accessed=moved, transcendentals=0),
    )(*args)


def dot(rows, weights):
    count = rows.shape[0]
    short = -count % TALL
    if short:
        rows = jnp.concatenate([rows, jnp.zeros((short, rows.shape[1]), rows.dtype)], axis=0)
    return jnp.dot(rows, weights, preferred_element_type=jnp.float32)[:count]


def scaled(rows):
    return rows * lax.rsqrt(jnp.mean(rows * rows, axis=1, keepdims=True) + 1e-05)


def own_kernel(rows_ref, out_ref):
    out_ref[...] = scaled(rows_ref[0])


def normalise_kernel(order, own_ref, *refs):
    *block_refs, out_ref = refs
    rows = [own_ref[...]] + [scaled(block_refs[order.index(j)][0]) for j in sorted(order)]
    out_ref[...] = jnp.concatenate(rows, axis=0).astype(jnp.bfloat16)


def stack_kernel(*refs):
    *block_refs, out_ref = refs
    whole = jnp.concatenate([ref[...].astype(jnp.float32) for ref in block_refs], axis=0)
    out_ref[...] = whole.astype(jnp.bfloat16)


def encode_kernel(*refs):
    *block_refs, enc_ref, bias_ref, limit_ref, dec_ref, codes_ref, own_ref = refs
    rows = jnp.concatenate([ref[...] for ref in block_refs], axis=0)
    pre = dot(rows, enc_ref[0]) + bias_ref[...]
    codes = (pre * jax.nn.sigmoid((pre - limit_ref[...]) / 0.1)).astype(jnp.bfloat16)
    codes_ref[...] = codes

    @pl.when(lax.axis_index("layer") % 2 == 1)
    def _():
        own_ref[...] = dot(codes, dec_ref[0])


def decode_kernel(codes_ref, dec_ref, early_ref, own_ref):
    @pl.when(lax.axis_index("layer") % 2 == 0)
    def _():
        own_ref[...] = dot(codes_ref[...], dec_ref[0])


def cut(total, part_refs):
    size = part_refs[0].shape[0]
    for i, part_ref in enumerate(part_refs):
        part_ref[...] = total[i * size : (i + 1) * size].astype(jnp.bfloat16)


def join_kernel(places, own_ref, before_ref, dec_ref, *part_refs):
    first = lax.axis_index("layer") == 0

    @pl.when(first)
    def _():
        cut(own_ref[...], part_refs)

    @pl.when(jnp.logical_not(first))
    def _():
        carried = dot(before_ref[...], dec_ref[0])
        block = carried.shape[0] // len(places)
        carried = jnp.concatenate([carried[i * block : (i + 1) * block] for i in places], axis=0)
        cut(own_ref[...] + carried, part_refs)


def added(block_refs):
    return sum(ref[...].astype(jnp.float32) for ref in block_refs)


def split_kernel(count, *refs):
    cut(added(refs[:count]), refs[count:])


def finish_kernel(*refs):
    *block_refs, target_ref, out_ref = refs
    out_ref[0] = added(block_refs) - target_ref[0]


def digits(count):
    assert count & (count - 1) == 0
    found, stride = [], 1
    while stride < count:
        radix = min(RADIX, count // stride)
        found.append((stride, radix))
        stride *= radix
    return found or [(1, 1)]


def body(source, w_enc, b_enc, threshold, dec_self, dec_next, target):
    feats = lax.axis_size("feat")
    layers = lax.axis_size("layer")
    _, block, depth = source.shape
    width = w_enc.shape[2]
    rows = feats * block
    work = 2 * rows * depth * width
    half, full = jnp.bfloat16, jnp.float32
    shape = jax.ShapeDtypeStruct
    steps = digits(feats)

    radices = [radix for _, radix in steps]
    turned = radices == radices[::-1]
    strides = [[stride for stride, _ in steps]] * 2
    if turned:
        strides = [strides[0], strides[0][::-1]]
    places = np.arange(feats).reshape(radices)
    places = [int(i) for i in (places.T if turned else places).ravel()]

    def swap(value, stage, j):
        flips = [strides[k % 2][stage] * j for k in range(layers)]
        pairs = [(k * feats + i, k * feats + (i ^ flips[k])) for k in range(layers) for i in range(feats)]
        return lax.ppermute(value, ("layer", "feat"), pairs)

    def onward(value):
        return lax.ppermute(value, "layer", [(i, (i + 1) % layers) for i in range(layers)])

    arrived_dec = onward(dec_next)

    last, radix = len(steps) - 1, radices[-1]
    order = [radix - 1, *range(1, radix - 1)] if radix > 1 else []
    blocks = [swap(source, last, j) for j in order]
    own = call(own_kernel, shape((block, depth), full), (source,), 2**36, 2**27)
    size = radix * block
    kernel = functools.partial(normalise_kernel, order)
    blocks = [call(kernel, shape((size, depth), half), [own] + blocks, 2**34)]
    for stage in reversed(range(last)):
        if len(blocks) > 1:
            blocks = [call(stack_kernel, shape((size, depth), half), blocks, 2**34)]
        blocks += [swap(blocks[0], stage, j) for j in range(1, radices[stage])]
        size *= radices[stage]

    codes, early = call(encode_kernel, (shape((rows, width), half), shape((rows, depth), full)), (*blocks, w_enc, b_enc, threshold, dec_self), work)
    before = onward(codes)
    own = call(decode_kernel, shape((rows, depth), full), (codes, dec_self, early), work, aliases=[(2, 0)])

    size = rows // radices[0]
    kernel = functools.partial(join_kernel, places)
    parts = call(kernel, (shape((size, depth), half),) * radices[0], (own, before, arrived_dec), work)
    for stage, radix in enumerate(radices):
        blocks = [parts[0]] + [swap(parts[j], stage, j) for j in reversed(range(1, radix))]
        if stage < last:
            size //= radices[stage + 1]
            kernel = functools.partial(split_kernel, radix)
            parts = call(kernel, (shape((size, depth), half),) * radices[stage + 1], blocks)
    return call(finish_kernel, shape(target.shape, full), (*blocks, target))


def solution(mesh):
    return jax.shard_map(
        body,
        mesh=mesh,
        in_specs=(
            P("layer", "feat", None),
            P("layer", None, "feat"),
            P("layer", "feat"),
            P("layer", "feat"),
            P("layer", "feat", None),
            P("layer", "feat", None),
            P("layer", "feat", None),
        ),
        out_specs=P("layer", "feat", None),
        check_vma=False,
    )
```

```python
import functools

import jax
import jax.numpy as jnp
import numpy as np
from jax import lax
from jax.experimental import pallas as pl
from jax.experimental.pallas import tpu as pltpu
from jax.sharding import PartitionSpec as P

VMEM = pl.BlockSpec(memory_space=pltpu.VMEM)
GRANT = 8 * 2**20
RADIX = 4
TALL = 128


def call(kernel, out_shape, args, flops=0, moved=2**18):
    return pl.pallas_call(
        kernel,
        out_shape=out_shape,
        in_specs=[VMEM] * len(args),
        out_specs=jax.tree.map(lambda _: VMEM, out_shape),
        compiler_params=pltpu.CompilerParams(vmem_limit_bytes=GRANT),
        cost_estimate=pl.CostEstimate(flops=flops, bytes_accessed=moved, transcendentals=0),
    )(*args)


def dot(rows, weights):
    count = rows.shape[0]
    short = -count % TALL
    if short:
        rows = jnp.concatenate([rows, jnp.zeros((short, rows.shape[1]), rows.dtype)], axis=0)
    return jnp.dot(rows, weights, preferred_element_type=jnp.float32)[:count]


def scaled(rows):
    return rows * lax.rsqrt(jnp.mean(rows * rows, axis=1, keepdims=True) + 1e-05)


def own_kernel(rows_ref, out_ref):
    out_ref[...] = scaled(rows_ref[0])


def normalise_kernel(order, own_ref, *refs):
    *block_refs, out_ref = refs
    arrived = [ref[...] if i == 0 else scaled(ref[0]) for i, ref in enumerate(block_refs)]
    rows = [own_ref[...]] + [arrived[order.index(j)] for j in sorted(order)]
    out_ref[...] = jnp.concatenate(rows, axis=0).astype(jnp.bfloat16)


def stack_kernel(*refs):
    *block_refs, out_ref = refs
    whole = jnp.concatenate([ref[...].astype(jnp.float32) for ref in block_refs], axis=0)
    out_ref[...] = whole.astype(jnp.bfloat16)


def encode_kernel(*refs):
    *block_refs, enc_ref, bias_ref, limit_ref, codes_ref = refs
    rows = jnp.concatenate([ref[...] for ref in block_refs], axis=0)
    pre = dot(rows, enc_ref[0]) + bias_ref[...]
    codes_ref[...] = (pre * jax.nn.sigmoid((pre - limit_ref[...]) / 0.1)).astype(jnp.bfloat16)


def decode_kernel(codes_ref, dec_ref, own_ref):
    own_ref[...] = dot(codes_ref[...], dec_ref[0])


def cut(total, part_refs):
    size = part_refs[0].shape[0]
    for i, part_ref in enumerate(part_refs):
        part_ref[...] = total[i * size : (i + 1) * size].astype(jnp.bfloat16)


def join_kernel(places, own_ref, before_ref, dec_ref, *part_refs):
    first = lax.axis_index("layer") == 0

    @pl.when(first)
    def _():
        cut(own_ref[...], part_refs)

    @pl.when(jnp.logical_not(first))
    def _():
        carried = dot(before_ref[...], dec_ref[0])
        block = carried.shape[0] // len(places)
        carried = jnp.concatenate([carried[i * block : (i + 1) * block] for i in places], axis=0)
        cut(own_ref[...] + carried, part_refs)


def added(block_refs):
    return sum(ref[...].astype(jnp.float32) for ref in block_refs)


def split_kernel(count, *refs):
    cut(added(refs[:count]), refs[count:])


def finish_kernel(*refs):
    *block_refs, target_ref, out_ref = refs
    out_ref[0] = added(block_refs) - target_ref[0]


def digits(count):
    assert count & (count - 1) == 0
    found, stride = [], 1
    while stride < count:
        radix = min(RADIX, count // stride)
        found.append((stride, radix))
        stride *= radix
    return found or [(1, 1)]


def body(source, w_enc, b_enc, threshold, dec_self, dec_next, target):
    feats = lax.axis_size("feat")
    layers = lax.axis_size("layer")
    _, block, depth = source.shape
    width = w_enc.shape[2]
    rows = feats * block
    work = 2 * rows * depth * width
    half, full = jnp.bfloat16, jnp.float32
    shape = jax.ShapeDtypeStruct
    steps = digits(feats)

    radices = [radix for _, radix in steps]
    turned = radices == radices[::-1]
    strides = [[stride for stride, _ in steps]] * 2
    if turned:
        strides = [strides[0], strides[0][::-1]]
    places = np.arange(feats).reshape(radices)
    places = [int(i) for i in (places.T if turned else places).ravel()]

    def swap(value, stage, j):
        flips = [strides[k % 2][stage] * j for k in range(layers)]
        pairs = [(k * feats + i, k * feats + (i ^ flips[k])) for k in range(layers) for i in range(feats)]
        return lax.ppermute(value, ("layer", "feat"), pairs)

    def onward(value):
        return lax.ppermute(value, "layer", [(i, (i + 1) % layers) for i in range(layers)])

    arrived_dec = onward(dec_next)

    last, radix = len(steps) - 1, radices[-1]
    order = [radix - 1, *range(1, radix - 1)] if radix > 1 else []
    blocks = [swap(source, last, j) for j in order]
    own = call(own_kernel, shape((block, depth), full), (source,), 2**36, 2**27)
    blocks[:1] = [call(own_kernel, shape((block, depth), full), (rows_of,)) for rows_of in blocks[:1]]
    size = radix * block
    kernel = functools.partial(normalise_kernel, order)
    blocks = [call(kernel, shape((size, depth), half), [own] + blocks, 2**34)]
    for stage in reversed(range(last)):
        if len(blocks) > 1:
            blocks = [call(stack_kernel, shape((size, depth), half), blocks, 2**34)]
        blocks += [swap(blocks[0], stage, j) for j in range(1, radices[stage])]
        size *= radices[stage]

    codes = call(encode_kernel, shape((rows, width), half), (*blocks, w_enc, b_enc, threshold), work)
    before = onward(codes)
    own = call(decode_kernel, shape((rows, depth), full), (codes, dec_self), work)

    size = rows // radices[0]
    kernel = functools.partial(join_kernel, places)
    parts = call(kernel, (shape((size, depth), half),) * radices[0], (own, before, arrived_dec), work)
    for stage, radix in enumerate(radices):
        blocks = [parts[0]] + [swap(parts[j], stage, j) for j in reversed(range(1, radix))]
        if stage < last:
            size //= radices[stage + 1]
            kernel = functools.partial(split_kernel, radix)
            parts = call(kernel, (shape((size, depth), half),) * radices[stage + 1], blocks)
    return call(finish_kernel, shape(target.shape, full), (*blocks, target))


def solution(mesh):
    return jax.shard_map(
        body,
        mesh=mesh,
        in_specs=(
            P("layer", "feat", None),
            P("layer", None, "feat"),
            P("layer", "feat"),
            P("layer", "feat"),
            P("layer", "feat", None),
            P("layer", "feat", None),
            P("layer", "feat", None),
        ),
        out_specs=P("layer", "feat", None),
        check_vma=False,
    )
```

```python
import functools

import jax
import jax.numpy as jnp
import numpy as np
from jax import lax
from jax.experimental import pallas as pl
from jax.experimental.pallas import tpu as pltpu
from jax.sharding import PartitionSpec as P

VMEM = pl.BlockSpec(memory_space=pltpu.VMEM)
GRANT = 8 * 2**20
RADIX = 4
TALL = 128


def call(kernel, out_shape, args, flops=0, moved=2**18, aliases={}):
    return pl.pallas_call(
        kernel,
        out_shape=out_shape,
        input_output_aliases=aliases,
        in_specs=[VMEM] * len(args),
        out_specs=jax.tree.map(lambda _: VMEM, out_shape),
        compiler_params=pltpu.CompilerParams(vmem_limit_bytes=GRANT),
        cost_estimate=pl.CostEstimate(flops=flops, bytes_accessed=moved, transcendentals=0),
    )(*args)


def dot(rows, weights):
    count = rows.shape[0]
    short = -count % TALL
    if short:
        rows = jnp.concatenate([rows, jnp.zeros((short, rows.shape[1]), rows.dtype)], axis=0)
    return jnp.dot(rows, weights, preferred_element_type=jnp.float32)[:count]


def scaled(rows):
    return rows * lax.rsqrt(jnp.mean(rows * rows, axis=1, keepdims=True) + 1e-05)


def own_kernel(rows_ref, out_ref):
    out_ref[...] = scaled(rows_ref[0])


def normalise_kernel(order, own_ref, *refs):
    *block_refs, out_ref = refs
    rows = [own_ref[...]] + [scaled(block_refs[order.index(j)][0]) for j in sorted(order)]
    out_ref[...] = jnp.concatenate(rows, axis=0).astype(jnp.bfloat16)


def stack_kernel(*refs):
    *block_refs, out_ref = refs
    whole = jnp.concatenate([ref[...].astype(jnp.float32) for ref in block_refs], axis=0)
    out_ref[...] = whole.astype(jnp.bfloat16)


def encode_kernel(*refs):
    *block_refs, enc_ref, bias_ref, limit_ref, codes_ref = refs
    rows = jnp.concatenate([ref[...] for ref in block_refs], axis=0)
    pre = dot(rows, enc_ref[0]) + bias_ref[...]
    codes_ref[...] = (pre * jax.nn.sigmoid((pre - limit_ref[...]) / 0.1)).astype(jnp.bfloat16)


def decode_kernel(codes_ref, dec_ref, own_ref, *part_refs):
    first = lax.axis_index("layer") == 0

    @pl.when(first)
    def _():
        cut(dot(codes_ref[...], dec_ref[0]), part_refs)

    @pl.when(jnp.logical_not(first))
    def _():
        own_ref[...] = dot(codes_ref[...], dec_ref[0])


def cut(total, part_refs):
    size = part_refs[0].shape[0]
    for i, part_ref in enumerate(part_refs):
        part_ref[...] = total[i * size : (i + 1) * size].astype(jnp.bfloat16)


def join_kernel(places, own_ref, before_ref, dec_ref, *refs):
    part_refs = refs[len(refs) // 2 :]

    @pl.when(lax.axis_index("layer") > 0)
    def _():
        carried = dot(before_ref[...], dec_ref[0])
        block = carried.shape[0] // len(places)
        carried = jnp.concatenate([carried[i * block : (i + 1) * block] for i in places], axis=0)
        cut(own_ref[...] + carried, part_refs)


def added(block_refs):
    return sum(ref[...].astype(jnp.float32) for ref in block_refs)


def gather_up_kernel(*refs):
    *block_refs, out_ref = refs
    out_ref[...] = added(block_refs)


def split_kernel(count, *refs):
    cut(added(refs[:count]), refs[count:])


def finish_kernel(*refs):
    *block_refs, target_ref, out_ref = refs
    out_ref[0] = added(block_refs) - target_ref[0]


def digits(count):
    assert count & (count - 1) == 0
    found, stride = [], 1
    while stride < count:
        radix = min(RADIX, count // stride)
        found.append((stride, radix))
        stride *= radix
    return found or [(1, 1)]


def body(source, w_enc, b_enc, threshold, dec_self, dec_next, target):
    feats = lax.axis_size("feat")
    layers = lax.axis_size("layer")
    _, block, depth = source.shape
    width = w_enc.shape[2]
    rows = feats * block
    work = 2 * rows * depth * width
    half, full = jnp.bfloat16, jnp.float32
    shape = jax.ShapeDtypeStruct
    steps = digits(feats)

    radices = [radix for _, radix in steps]
    turned = radices == radices[::-1]
    strides = [[stride for stride, _ in steps]] * 2
    if turned:
        strides = [strides[0], strides[0][::-1]]
    places = np.arange(feats).reshape(radices)
    places = [int(i) for i in (places.T if turned else places).ravel()]

    def swap(value, stage, j):
        flips = [strides[k % 2][stage] * j for k in range(layers)]
        pairs = [(k * feats + i, k * feats + (i ^ flips[k])) for k in range(layers) for i in range(feats)]
        return lax.ppermute(value, ("layer", "feat"), pairs)

    def onward(value):
        return lax.ppermute(value, "layer", [(i, (i + 1) % layers) for i in range(layers)])

    arrived_dec = onward(dec_next)

    last, radix = len(steps) - 1, radices[-1]
    order = [radix - 1, *range(1, radix - 1)] if radix > 1 else []
    blocks = [swap(source, last, j) for j in order]
    own = call(own_kernel, shape((block, depth), full), (source,), 2**36, 2**27)
    size = radix * block
    kernel = functools.partial(normalise_kernel, order)
    blocks = [call(kernel, shape((size, depth), half), [own] + blocks, 2**34)]
    for stage in reversed(range(last)):
        if len(blocks) > 1:
            blocks = [call(stack_kernel, shape((size, depth), half), blocks, 2**34)]
        blocks += [swap(blocks[0], stage, j) for j in range(1, radices[stage])]
        size *= radices[stage]

    codes = call(encode_kernel, shape((rows, width), half), (*blocks, w_enc, b_enc, threshold), work)
    before = onward(codes)
    size = rows // radices[0]
    pieces = (shape((size, depth), half),) * radices[0]
    own, *parts = call(decode_kernel, (shape((rows, depth), full), *pieces), (codes, dec_self), work)
    kernel = functools.partial(join_kernel, places)
    parts = call(kernel, pieces, (own, before, arrived_dec, *parts), work, aliases={3 + i: i for i in range(radices[0])})
    for stage, radix in enumerate(radices):
        blocks = [parts[0]] + [swap(parts[j], stage, j) for j in reversed(range(1, radix))]
        if stage < last:
            size //= radices[stage + 1]
            kernel = functools.partial(split_kernel, radix)
            parts = call(kernel, (shape((size, depth), half),) * radices[stage + 1], blocks)
    return call(finish_kernel, shape(target.shape, full), (*blocks, target))


def solution(mesh):
    return jax.shard_map(
        body,
        mesh=mesh,
        in_specs=(
            P("layer", "feat", None),
            P("layer", None, "feat"),
            P("layer", "feat"),
            P("layer", "feat"),
            P("layer", "feat", None),
            P("layer", "feat", None),
            P("layer", "feat", None),
        ),
        out_specs=P("layer", "feat", None),
        check_vma=False,
    )
```

```python
import functools

import jax
import jax.numpy as jnp
import numpy as np
from jax import lax
from jax.experimental import pallas as pl
from jax.experimental.pallas import tpu as pltpu
from jax.sharding import PartitionSpec as P

VMEM = pl.BlockSpec(memory_space=pltpu.VMEM)
GRANT = 8 * 2**20
RADIX = 4
TALL = 128


def call(kernel, out_shape, args, flops=0, moved=2**18):
    return pl.pallas_call(
        kernel,
        out_shape=out_shape,
        in_specs=[VMEM] * len(args),
        out_specs=jax.tree.map(lambda _: VMEM, out_shape),
        compiler_params=pltpu.CompilerParams(vmem_limit_bytes=GRANT),
        cost_estimate=pl.CostEstimate(flops=flops, bytes_accessed=moved, transcendentals=0),
    )(*args)


def dot(rows, weights):
    count = rows.shape[0]
    short = -count % TALL
    if short:
        rows = jnp.concatenate([rows, jnp.zeros((short, rows.shape[1]), rows.dtype)], axis=0)
    return jnp.dot(rows, weights, preferred_element_type=jnp.float32)[:count]


def scaled(rows):
    return rows * lax.rsqrt(jnp.mean(rows * rows, axis=1, keepdims=True) + 1e-05)


def own_kernel(rows_ref, out_ref):
    out_ref[...] = scaled(rows_ref[0])


def normalise_kernel(order, own_ref, *refs):
    *block_refs, out_ref = refs
    rows = [own_ref[...]] + [scaled(block_refs[order.index(j)][0]) for j in sorted(order)]
    out_ref[...] = jnp.concatenate(rows, axis=0).astype(jnp.bfloat16)


def stack_kernel(*refs):
    *block_refs, out_ref = refs
    whole = jnp.concatenate([ref[...].astype(jnp.float32) for ref in block_refs], axis=0)
    out_ref[...] = whole.astype(jnp.bfloat16)


def encode_kernel(*refs):
    *block_refs, enc_ref, bias_ref, limit_ref, codes_ref = refs
    rows = jnp.concatenate([ref[...] for ref in block_refs], axis=0)
    pre = dot(rows, enc_ref[0]) + bias_ref[...]
    codes_ref[...] = (pre * jax.nn.sigmoid((pre - limit_ref[...]) / 0.1)).astype(jnp.bfloat16)


def decode_kernel(codes_ref, dec_ref, own_ref):
    own_ref[...] = dot(codes_ref[...], dec_ref[0])


def cut(total, part_refs):
    size = part_refs[0].shape[0]
    for i, part_ref in enumerate(part_refs):
        part_ref[...] = total[i * size : (i + 1) * size].astype(jnp.bfloat16)


def join_kernel(places, own_ref, before_ref, dec_ref, *part_refs):
    first = lax.axis_index("layer") == 0

    @pl.when(first)
    def _():
        cut(own_ref[...], part_refs)

    @pl.when(jnp.logical_not(first))
    def _():
        carried = dot(before_ref[...], dec_ref[0])
        block = carried.shape[0] // len(places)
        carried = jnp.concatenate([carried[i * block : (i + 1) * block] for i in places], axis=0)
        cut(own_ref[...] + carried, part_refs)


def added(block_refs):
    return sum(ref[...].astype(jnp.float32) for ref in block_refs)


def split_kernel(count, *refs):
    cut(added(refs[:count]), refs[count:])


def finish_kernel(*refs):
    *block_refs, target_ref, out_ref = refs
    out_ref[0] = added(block_refs) - target_ref[0]


def digits(count):
    assert count & (count - 1) == 0
    found, stride = [], 1
    while stride < count:
        radix = min(RADIX, count // stride)
        found.append((stride, radix))
        stride *= radix
    return found or [(1, 1)]


def body(source, w_enc, b_enc, threshold, dec_self, dec_next, target):
    feats = lax.axis_size("feat")
    layers = lax.axis_size("layer")
    _, block, depth = source.shape
    width = w_enc.shape[2]
    rows = feats * block
    work = 2 * rows * depth * width
    half, full = jnp.bfloat16, jnp.float32
    shape = jax.ShapeDtypeStruct
    steps = digits(feats)

    radices = [radix for _, radix in steps]
    turned = radices == radices[::-1]
    strides = [[stride for stride, _ in steps]] * 2
    if turned:
        strides = [strides[0], strides[0][::-1]]
    places = np.arange(feats).reshape(radices)
    places = [int(i) for i in (places.T if turned else places).ravel()]

    def swap(value, stage, j):
        flips = [strides[k % 2][stage] * j for k in range(layers)]
        pairs = [(k * feats + i, k * feats + (i ^ flips[k])) for k in range(layers) for i in range(feats)]
        return lax.ppermute(value, ("layer", "feat"), pairs)

    def onward(value):
        return lax.ppermute(value, "layer", [(i, (i + 1) % layers) for i in range(layers)])

    arrived_dec = onward(dec_next)

    last, radix = len(steps) - 1, radices[-1]
    order = [radix - 1, *range(1, radix - 1)] if radix > 1 else []
    blocks = [swap(source, last, j) for j in order]
    own = call(own_kernel, shape((block, depth), full), (source,), 2**34, 2**25)
    size = radix * block
    kernel = functools.partial(normalise_kernel, order)
    blocks = [call(kernel, shape((size, depth), half), [own] + blocks, 2**34)]
    for stage in reversed(range(last)):
        if len(blocks) > 1:
            blocks = [call(stack_kernel, shape((size, depth), half), blocks, 2**34)]
        blocks += [swap(blocks[0], stage, j) for j in range(1, radices[stage])]
        size *= radices[stage]

    codes = call(encode_kernel, shape((rows, width), half), (*blocks, w_enc, b_enc, threshold), work)
    before = onward(codes)
    own = call(decode_kernel, shape((rows, depth), full), (codes, dec_self), work)

    size = rows // radices[0]
    kernel = functools.partial(join_kernel, places)
    parts = call(kernel, (shape((size, depth), half),) * radices[0], (own, before, arrived_dec), work)
    for stage, radix in enumerate(radices):
        blocks = [parts[0]] + [swap(parts[j], stage, j) for j in reversed(range(1, radix))]
        if stage < last:
            size //= radices[stage + 1]
            kernel = functools.partial(split_kernel, radix)
            parts = call(kernel, (shape((size, depth), half),) * radices[stage + 1], blocks)
    return call(finish_kernel, shape(target.shape, full), (*blocks, target))


def solution(mesh):
    return jax.shard_map(
        body,
        mesh=mesh,
        in_specs=(
            P("layer", "feat", None),
            P("layer", None, "feat"),
            P("layer", "feat"),
            P("layer", "feat"),
            P("layer", "feat", None),
            P("layer", "feat", None),
            P("layer", "feat", None),
        ),
        out_specs=P("layer", "feat", None),
        check_vma=False,
    )
```
